512 devices in a mesh: ep: 128 (over x, z, core), tp: 4 (over y).
Axes of the slice: x: 4, y: 4, z: 16, core: 2. Of those that a mesh axis runs over, the one named last changes fastest.
Arguments:
- grad_out: bfloat16 [16384, 2048], P('ep'), may hold values from -6 to 6
- expert_ids: int32 [16384, 10], P('ep'), may hold values from 0 to 255, all different within a row; in each aligned block of 128 rows (0 to 127, 128 to 255, ...) at most 6 rows name the same one
- gate_values: float32 [16384, 10], P('ep'), may hold values from 0.04 to 0.24
- saved_gate_up: bfloat16 [256, 2, 768, 512], P('ep', None, None, 'tp'), may hold values from -6 to 6
- expert_gate_up: bfloat16 [256, 2, 2048, 512], P('ep', None, None, 'tp'), may hold values from -0.25 to 0.25
- expert_down: bfloat16 [256, 512, 2048], P('ep', 'tp'), may hold values from -0.125 to 0.125
- shared_saved: bfloat16 [2, 16384, 512], P(None, 'ep', 'tp'), may hold values from -6 to 6
- shared_gate_up: bfloat16 [2, 2048, 512], P(None, 'ep', 'tp'), may hold values from -0.25 to 0.25
- shared_down: bfloat16 [512, 2048], P('tp', 'ep'), may hold values from -0.125 to 0.125
Outputs:
- grad_in: bfloat16 [16384, 2048], P('ep', 'tp')
The draws below stay inside these ranges and needn't reach their ends.
Inputs may be any that keep to these rules, and one draw needn't show every extreme that they name: `expert_ids`: each token names 10 different experts; among the 128 tokens of one index of ep no expert is named more than 6 times, a bound that some block reaches.
All inputs are finite; a program needn't handle non-finite values.
Results may differ from the reference program's by a relative error of at most 0.0051.
Values may be sent and summed in bfloat16 or wider, within the bound.
A program may use at most 128 MiB of HBM per device.

```python
import math
import jax
import jax.numpy as jnp
import numpy as np
from jax import lax

D = 2048
FFE = 512
FFS = 512
TOP = 10
TOK_DEV = 128
EXPERTS = 256
TOKENS = 16384
CAP = 6
SLOTS = 768
N_EP = 128
N_TP = 4


def block_scale(own_key, extent, shards, low, largest):
    level = 1.0
    for position, shards_of in shards:
        draws = jax.random.uniform(jax.random.fold_in(jax.random.fold_in(own_key, 6), position), (shards_of,), jnp.float32, low / len(shards), largest / len(shards))
        level = level * jnp.repeat(jnp.exp(draws), extent[position] // shards_of).reshape((-1,) + (1,) * (len(extent) - 1 - position))
    return level


def routed_block(stream_key, own, number, rows, number_of, top, most, slope):
    ranking = jax.random.permutation(stream_key, number_of)
    crowded, common = load_shares(number_of, rows * top, most, slope, True), load_shares(number_of, rows * top, most, slope, False)
    places = jnp.arange(number_of)

    def named(sizes, rotation):
        used = int((sizes > 0).sum())
        fixed = max(1, used // 4)
        moved = fixed + (places - fixed + rotation * (used - fixed)) % max(1, number_of - fixed)
        return jnp.zeros((number_of,), jnp.int32).at[ranking[jnp.where(places < fixed, places, moved)]].set(jnp.asarray(sizes, jnp.int32))

    sizes = jnp.where(number % 4 == 0, named(crowded, number // 4), named(common, number - number // 4 - 1))
    mixed = jax.random.permutation(jax.random.fold_in(own, 3), number_of)
    donor, receiver = mixed[0:number_of // 2 * 2:2], mixed[1:number_of // 2 * 2:2]
    room = jnp.minimum(sizes[donor] - 1, most - sizes[receiver]) // 2
    room = jnp.where((donor == ranking[0]) | (receiver == ranking[0]) | (sizes[receiver] == 0), 0, jnp.maximum(room, 0))
    moved = jax.random.randint(jax.random.fold_in(own, 4), (number_of // 2,), 0, 1 << 20) % (room + 1)
    sizes = sizes.at[donor].add(-moved).at[receiver].add(moved)
    items = jnp.searchsorted(jnp.cumsum(sizes), jnp.arange(rows * top), side="right").astype(jnp.int32)
    table = items.reshape(top, rows).T
    table = table[jax.random.permutation(jax.random.fold_in(own, 1), rows)]
    rotation = jax.random.randint(jax.random.fold_in(own, 2), (rows, 1), 0, top)
    return jnp.take_along_axis(table, (jnp.arange(top)[None, :] + rotation) % top, axis=1)


def load_shares(amount, total, bound, slope, full):
    weights = [(1 << 20) // math.isqrt(standing ** slope) + 1 for standing in range(1, amount + 1)]
    largest = bound if full else min(bound, max(-(-total // amount), total * weights[0] // sum(weights)))
    least = 1 if total - largest >= amount - 1 else 0
    given, spare = [largest] + [least] * (amount - 1), total - largest - least * (amount - 1)
    while spare > 0:
        candidates = [i for i in range(1, amount) if given[i] < largest] or [i for i in range(1, amount) if given[i] < bound]
        mass, left = sum([weights[i] for i in candidates]), spare
        for i in candidates:
            extra = min(bound - given[i], max(1, left * weights[i] // mass), spare)
            given[i] = given[i] + extra
            spare = spare - extra
    return np.array(given)


def normal_values(rng, dims, spread, reach, split=(), held_as=jnp.bfloat16):
    entries = spread * jax.random.normal(rng, dims, jnp.float32)
    if split:
        entries = entries * block_scale(rng, dims, split, -0.22, 0.18)
    return jnp.clip(entries, -reach, reach).astype(held_as)


def setup_inputs(seed: int = 0) -> dict:
    keys = jax.random.split(jax.random.key(seed), 10)
    grad_out = normal_values(keys[0], (TOKENS, D), 1.0, 6.0, ((0, 128),))
    expert_ids_keys = jax.random.split(jax.random.fold_in(keys[1], 1), TOKENS // TOK_DEV)
    expert_ids_turns = jax.random.permutation(jax.random.fold_in(keys[1], 3), TOKENS // TOK_DEV)
    expert_ids = jax.vmap(lambda own, number: routed_block(jax.random.fold_in(keys[1], 2), own, number, TOK_DEV, EXPERTS, TOP, CAP, 2))(expert_ids_keys, expert_ids_turns).reshape((TOKENS, TOP))
    gate_values = jnp.clip(0.04 + 0.19999999552965164 * jax.random.uniform(keys[2], (TOKENS, TOP), jnp.float32) ** block_scale(keys[2], (TOKENS, TOP), ((0, 128),), -0.2, 0.2), 0.04, 0.24)
    saved_gate_up = normal_values(keys[3], (EXPERTS, 2, SLOTS, FFE), 1.0, 6.0, ((0, 128), (3, 4)))
    expert_gate_up = normal_values(keys[4], (EXPERTS, 2, D, FFE), FFE ** -0.5, 0.25, ((0, 128), (3, 4)))
    expert_down = normal_values(keys[5], (EXPERTS, FFE, D), D ** -0.5, 0.125, ((0, 128), (1, 4)))
    shared_saved = normal_values(keys[6], (2, TOKENS, FFS), 1.0, 6.0, ((1, 128), (2, 4)))
    shared_gate_up = normal_values(keys[7], (2, D, FFS), FFS ** -0.5, 0.25, ((1, 128), (2, 4)))
    shared_down = normal_values(keys[8], (FFS, D), D ** -0.5, 0.125, ((0, 4), (1, 128)))
    return dict(grad_out=grad_out, expert_ids=expert_ids, gate_values=gate_values, saved_gate_up=saved_gate_up, expert_gate_up=expert_gate_up, expert_down=expert_down, shared_saved=shared_saved, shared_gate_up=shared_gate_up, shared_down=shared_down)


def block_ranks(block_ids):
    flat_ids = block_ids.reshape(-1)
    one_hot = (flat_ids[:, None] == jnp.arange(EXPERTS, dtype=jnp.int32)[None, :]).astype(jnp.int32)
    return lax.optimization_barrier(jnp.sum((jnp.cumsum(one_hot, axis=0) - one_hot) * one_hot, axis=1)).astype(jnp.int32)

def activation_grad(hidden_grad, saved_pair):
    gate_pre = saved_pair[0].astype(jnp.float32)
    up_pre = saved_pair[1].astype(jnp.float32)
    squash = jax.nn.sigmoid(gate_pre)
    gate_grad = (hidden_grad * up_pre * squash * (1.0 + gate_pre * (1.0 - squash))).astype(jnp.bfloat16)
    up_grad = (hidden_grad * gate_pre * squash).astype(jnp.bfloat16)
    return (gate_grad, up_grad)

def reference(grad_out, expert_ids, gate_values, saved_gate_up, expert_gate_up, expert_down, shared_saved, shared_gate_up, shared_down):
    slot_ranks = lax.map(block_ranks, expert_ids.reshape(N_EP, TOK_DEV, TOP)).reshape(-1).astype(jnp.int32)
    flat_experts = expert_ids.reshape(-1).astype(jnp.int32)
    token_of = (jnp.arange(TOKENS * TOP, dtype=jnp.int32) // TOP).astype(jnp.int32)
    slot_pos = (token_of // TOK_DEV * CAP + slot_ranks).astype(jnp.int32)
    slot_token = jnp.zeros((EXPERTS, SLOTS), jnp.int32).at[flat_experts, slot_pos].set(token_of)
    slot_gate = jnp.zeros((EXPERTS, SLOTS), gate_values.dtype).at[flat_experts, slot_pos].set(gate_values.reshape(-1))
    group = FFE // N_TP

    def expert_step(accumulated, inputs):
        gate_up, down_rows, saved_pair, token_rows, weight = inputs
        expert_rows = grad_out[token_rows]
        hidden_grad = jnp.dot(expert_rows, down_rows.T, preferred_element_type=jnp.float32)
        gate_grad, up_grad = activation_grad(hidden_grad, saved_pair)
        gate_quart = gate_grad.astype(jnp.float32).reshape(SLOTS, N_TP, group)
        up_quart = up_grad.astype(jnp.float32).reshape(SLOTS, N_TP, group)
        gate_mat = gate_up[0].astype(jnp.float32).reshape(D, N_TP, group)
        up_mat = gate_up[1].astype(jnp.float32).reshape(D, N_TP, group)
        partial_value = jnp.einsum('sqf,dqf->qsd', gate_quart, gate_mat) + jnp.einsum('sqf,dqf->qsd', up_quart, up_mat)
        rounded = lax.optimization_barrier(partial_value.astype(jnp.bfloat16))
        summed = lax.optimization_barrier(jnp.sum(rounded.astype(jnp.float32), axis=0))
        accumulated = accumulated.at[token_rows].add(weight[:, None].astype(jnp.float32) * summed)
        return (accumulated, None)
    routed, _ = lax.scan(expert_step, jnp.zeros((TOKENS, D), jnp.float32), (expert_gate_up, expert_down, saved_gate_up, slot_token, slot_gate))
    shared_hidden = jnp.dot(grad_out, shared_down.T, preferred_element_type=jnp.float32)
    shared_gate_grad, shared_up_grad = activation_grad(shared_hidden, shared_saved)
    shared_part = jnp.dot(shared_gate_grad, shared_gate_up[0].T, preferred_element_type=jnp.float32) + jnp.dot(shared_up_grad, shared_gate_up[1].T, preferred_element_type=jnp.float32)
    return (routed + shared_part).astype(jnp.bfloat16)
```

```python
import functools

import jax
import jax.numpy as jnp
from jax import lax
from jax.experimental import pallas as pl
from jax.experimental.pallas import tpu as pltpu
from jax.sharding import PartitionSpec as P

BF = jnp.bfloat16
F32 = jnp.float32
NX, NZ, NC, NY = 4, 16, 2, 4
PEERS = NX * NC
TOK = 128
CAP = 6
TOP = 10
DQ = 512
HQ = 128
NE = 2
GROUPS = 2
SPAN = NZ // GROUPS
SROWS = SPAN * CAP
QN = PEERS * NE
ROWS = PEERS * SROWS
HOME = 3


def dot_nt(a, b):
    return lax.dot_general(a, b, (((1,), (1,)), ((), ())), preferred_element_type=F32)


def dot_nn(a, b):
    return lax.dot_general(a, b, (((1,), (0,)), ((), ())), preferred_element_type=F32)


def dot_tn(a, b):
    return lax.dot_general(a, b, (((0,), (0,)), ((), ())), preferred_element_type=F32)


def act_grad(h, g, u):
    g = g.astype(F32)
    u = u.astype(F32)
    s = jax.nn.sigmoid(g)
    return (h * u * s * (1.0 + g * (1.0 - s))).astype(BF), (h * g * s).astype(BF)


def kernel(
    x_in, meta_in, sw_in, saved, gu, down, ssaved, out,
    XG, MG, SW, SEL, WTH, WTL, SB, R1, W1, W2, SVI, SVP, HO, HS, HR, G, OB, BK, PT, ZS, ZR, XF, SHO, SP, SR,
    ssem, rsem, lsem,
):
    ep = lax.axis_index("ep")
    y = lax.axis_index("tp")
    c = lax.rem(ep, NC)
    z = lax.rem(lax.div(ep, NC), NZ)
    x = lax.div(ep, NC * NZ)
    me = x * NC + c

    def zdev(off):
        return ((x * NZ + lax.rem(z + off + NZ, NZ)) * NC + c, y)

    def pdev(peer):
        return ((lax.div(peer, NC) * NZ + z) * NC + lax.rem(peer, NC), y)

    def peer_of(d):
        return lax.rem(me + d + PEERS, PEERS)

    def yof(d):
        return lax.rem(y + d + NY, NY)

    def ydev(d):
        return (ep, yof(d))

    counts = {"s": 0, "r": 0, "l": 0}
    pending = []

    def rsem_new():
        counts["r"] += 1
        return rsem.at[counts["r"] - 1]

    def send(src, dst, rs, dev):
        ss = ssem.at[counts["s"]]
        counts["s"] += 1
        cp = pltpu.make_async_remote_copy(
            src_ref=src, dst_ref=dst, send_sem=ss, recv_sem=rs, device_id=dev,
            device_id_type=pl.DeviceIdType.MESH,
        )
        cp.start()
        pending.append(cp)

    def recv(dst, rs):
        pltpu.make_async_remote_copy(
            src_ref=dst, dst_ref=dst, send_sem=rs, recv_sem=rs, device_id=(ep, y),
            device_id_type=pl.DeviceIdType.MESH,
        ).wait_recv()

    def local(src, dst):
        cp = pltpu.make_async_copy(src, dst, lsem.at[counts["l"]])
        counts["l"] += 1
        cp.start()
        return cp

    barrier = pltpu.get_barrier_semaphore()
    others = [zdev(1), zdev(-1)] + [pdev(peer_of(d)) for d in range(1, PEERS)] + [ydev(d) for d in range(1, NY)]
    for dev in others:
        pl.semaphore_signal(barrier, inc=1, device_id=dev, device_id_type=pl.DeviceIdType.MESH)
    mine = pl.ds(pl.multiple_of(y * DQ, DQ), DQ)
    cp_x = local(x_in.at[:, mine], XG.at[HOME])
    cp_m = local(meta_in, MG.at[HOME])
    cp_s = local(sw_in, SW.at[:, x, z, c])
    cp_sv = [local(saved.at[e, k], SVI.at[:, pl.ds((2 * e + k) * HQ, HQ)]) for e in range(NE) for k in range(2)]
    cp_w1 = local(down.at[:, :, mine], W1.at[:, pl.ds(pl.multiple_of(y * HQ, HQ), HQ), :])
    cp_w2 = local(gu.at[:, :, mine, :], W2.at[:, y])
    cp_xf = local(x_in, XF)
    pl.semaphore_wait(barrier, len(others))

    def slot(off):
        return (off + HOME) % NZ

    ag_sems = {}

    def ag_refs(s, direction, at_sender):
        hops = s - 1 if at_sender else s
        off = -hops if direction == 0 else hops
        k = slot(off)
        zz = lax.rem(z + off + NZ, NZ)
        if s < 8:
            return [XG.at[k], MG.at[k], SW.at[:, x, zz, c]]
        if direction == 0:
            return [XG.at[k, :, pl.ds(0, DQ // 2)], MG.at[k], SW.at[:, x, zz, c]]
        return [XG.at[k, :, pl.ds(DQ // 2, DQ // 2)]]

    def ag_send(s):
        for direction in range(2):
            srcs = ag_refs(s, direction, True)
            if s == 1:
                srcs = [x_in.at[:, mine], meta_in, sw_in]
            landing = ag_refs(s, direction, False)
            off_there = -s if direction == 0 else s
            dev = zdev(1 if direction == 0 else -1)
            for i, src in enumerate(srcs):
                rs = rsem_new()
                ag_sems[(s, direction, i)] = rs
                k = slot(off_there)
                zz = lax.rem(z + (-(s - 1) if direction == 0 else s - 1) + NZ, NZ)
                dst = [XG.at[k], MG.at[k], SW.at[:, x, zz, c]][i]
                if s == 8 and i == 0:
                    dst = XG.at[k, :, pl.ds(direction * (DQ // 2), DQ // 2)]
                send(src, dst, rs, dev)

    def ag_recv(s):
        for direction in range(2):
            for i, ref in enumerate(ag_refs(s, direction, False)):
                recv(ref, ag_sems[(s, direction, i)])

    ag_send(1)

    w1_sems, w2_sems = {}, {}
    for d in range(1, NY):
        w1_sems[d] = rsem_new()
        there = pl.ds(pl.multiple_of(yof(d) * DQ, DQ), DQ)
        send(down.at[:, :, there], W1.at[:, pl.ds(pl.multiple_of(y * HQ, HQ), HQ), :], w1_sems[d], ydev(d))
    for d in range(1, NY):
        w2_sems[d] = rsem_new()
        there = pl.ds(pl.multiple_of(yof(d) * DQ, DQ), DQ)
        send(gu.at[:, :, there, :], W2.at[:, y], w2_sems[d], ydev(d))

    for cp in cp_sv:
        cp.wait()

    def permute_saved(g):
        shape = (PEERS, SROWS, NZ * PEERS * CAP)
        src = lax.broadcasted_iota(jnp.int32, shape, 0)
        i = lax.broadcasted_iota(jnp.int32, shape, 1)
        lane = lax.broadcasted_iota(jnp.int32, shape, 2)
        j = lax.shift_right_logical(i * 43, 8)
        zz = (z + j + (SPAN * g - HOME + NZ)) & (NZ - 1)
        target = lax.shift_right_logical(src, 1) * (NZ * NC * CAP) + zz * (NC * CAP) + (src & 1) * CAP + (i - j * CAP)
        pick = jnp.where(target == lane, 1.0, 0.0).astype(BF).reshape(ROWS, NZ * PEERS * CAP)
        SVP[g] = dot_nn(pick, SVI[...]).astype(BF)

    qi = lax.broadcasted_iota(jnp.int32, (QN, TOK), 0)
    expert = (lax.shift_right_logical(qi, 2) * (NZ * NC * NE) + z * (NC * NE) + (qi & 3)).astype(F32)
    before = jnp.where(
        lax.broadcasted_iota(jnp.int32, (TOK, TOK), 0) < lax.broadcasted_iota(jnp.int32, (TOK, TOK), 1), 1.0, 0.0
    ).astype(BF)
    row3 = lax.broadcasted_iota(jnp.int32, (QN, SROWS, TOK), 1).astype(F32)
    lane_q = lax.broadcasted_iota(jnp.int32, (QN, QN * SROWS), 1)
    row_q = lax.broadcasted_iota(jnp.int32, (QN, QN * SROWS), 0)
    in_q = (lane_q >= row_q * SROWS) & (lane_q < row_q * SROWS + SROWS)
    spread = jnp.where(in_q, 1.0, 0.0).astype(BF)
    lane_i = jnp.sum(jnp.where(in_q, lane_q - row_q * SROWS, 0).astype(F32), axis=0, keepdims=True)

    def place(k):
        meta = MG[k]
        named = jnp.zeros((QN, TOK), F32)
        gate = jnp.zeros((QN, TOK), F32)
        for i in range(TOP):
            hit = meta[i:i + 1, :] == expert
            named = jnp.where(hit, 1.0, named)
            gate = jnp.where(hit, meta[TOP + i:TOP + i + 1, :], gate)
        rank = dot_nn(named.astype(BF), before)
        key = jnp.where(named > 0.5, rank + float((k % SPAN) * CAP), -1.0)
        return key, gate

    x_sems, b_sems = {}, {}

    def select(g):
        for j in range(SPAN):
            key, gate = place(g * SPAN + j)
            hot = jnp.where(key[:, None, :] == row3, 1.0, 0.0).astype(BF)
            SEL[:, pl.ds(j * TOK, TOK)] = hot.reshape(QN * SROWS, TOK)
        rows = XG[g * SPAN:(g + 1) * SPAN].reshape(SPAN * TOK, DQ)
        half = QN * SROWS // 2
        for h in range(2):
            got = dot_nn(SEL[pl.ds(h * half, half), :], rows).astype(BF)
            SB[g, h * (QN // 2):(h + 1) * (QN // 2)] = got.reshape(QN // 2, SROWS, DQ)
        for d in range(1, PEERS):
            rs = rsem_new()
            x_sems[(g, d)] = rs
            peer = peer_of(d)
            send(SB.at[g, pl.ds(peer * NE, NE)], R1.at[g, :, me], rs, pdev(peer))
        return local(SB.at[g, pl.ds(me * NE, NE)], R1.at[g, :, me])

    def weigh(g):
        for j in range(SPAN):
            key, gate = place(g * SPAN + j)
            high = gate.astype(BF)
            low = (gate - high.astype(F32)).astype(BF)
            where = dot_tn(key.astype(BF), spread) == lane_i
            at = pl.ds(j * TOK, TOK)
            WTH[g, at, :] = jnp.where(where, dot_tn(high, spread), 0.0).astype(BF)
            WTL[g, at, :] = jnp.where(where, dot_tn(low, spread), 0.0).astype(BF)

    keep = {}
    cp_x.wait()
    cp_m.wait()
    cp_s.wait()
    for s in range(1, 9):
        ag_recv(s)
        if s < 8:
            ag_send(s + 1)
        if s == 2:
            permute_saved(0)
        if s == 3:
            permute_saved(1)
        if s == 4:
            keep[0] = select(0)
        if s == 5:
            weigh(0)

    sw_sems = {}
    keep[1] = select(1)
    for d in range(1, PEERS):
        sw_sems[d] = rsem_new()
        peer = peer_of(d)
        part = SW.at[:, x, :, c]
        send(part, part, sw_sems[d], pdev(peer))

    h_sems, g_sems = {}, {}
    cp_w1.wait()
    for d in range(1, NY):
        src = yof(-d)
        recv(W1.at[:, pl.ds(pl.multiple_of(src * HQ, HQ), HQ), :], w1_sems[d])

    def hidden(g):
        keep[g].wait()
        for d in range(1, PEERS):
            recv(R1.at[g, :, peer_of(-d)], x_sems[(g, d)])
        for e in range(NE):
            rows = R1[g, e].reshape(ROWS, DQ)
            for d in list(range(1, NY)) + [0]:
                q = yof(d)
                part = dot_nt(rows, W1[e, pl.ds(pl.multiple_of(q * HQ, HQ), HQ), :])
                if d == 0:
                    HO[g, e] = part
                else:
                    HS[g, e, d - 1] = part.astype(BF)
                    rs = rsem_new()
                    h_sems[(g, e, d)] = rs
                    send(HS.at[g, e, d - 1], HR.at[g, e, d - 1], rs, ydev(d))

    def activate(g):
        for e in range(NE):
            h = HO[g, e]
            for d in range(1, NY):
                recv(HR.at[g, e, d - 1], h_sems[(g, e, d)])
                h = h + HR[g, e, d - 1].astype(F32)
            gate_pre = SVP[g, :, pl.ds(2 * e * HQ, HQ)]
            up_pre = SVP[g, :, pl.ds((2 * e + 1) * HQ, HQ)]
            a, b = act_grad(h, gate_pre, up_pre)
            G[g, e, y, 0] = a
            G[g, e, y, 1] = b
            for d in range(1, NY):
                rs = rsem_new()
                g_sems[(g, e, d)] = rs
                send(G.at[g, e, y], G.at[g, e, y], rs, ydev(d))

    def outward(g):
        for e in range(NE):
            for d in range(1, NY):
                recv(G.at[g, e, yof(-d)], g_sems[(g, e, d)])
            left = jnp.concatenate([G[g, e, q, k] for q in range(NY) for k in range(2)], axis=1)
            right = jnp.concatenate([W2[e, q, k] for q in range(NY) for k in range(2)], axis=1)
            OB[g, e] = dot_nt(left, right).astype(BF).reshape(PEERS, SROWS, DQ)
        for d in range(1, PEERS):
            rs = rsem_new()
            b_sems[(g, d)] = rs
            peer = peer_of(d)
            send(OB.at[g, :, peer], BK.at[g, pl.ds(me * NE, NE)], rs, pdev(peer))
        return local(OB.at[g, :, me], BK.at[g, pl.ds(me * NE, NE)])

    def combine(g):
        keep[g + 2].wait()
        for d in range(1, PEERS):
            recv(BK.at[g, pl.ds(peer_of(-d) * NE, NE)], b_sems[(g, d)])
        rows = BK[g].reshape(QN * SROWS, DQ)
        n = 4
        size = SPAN * TOK // n
        for i in range(n):
            at = pl.ds(i * size, size)
            got = dot_nn(WTH[g, at, :], rows) + dot_nn(WTL[g, at, :], rows)
            PT[g * SPAN + i * (SPAN // n):g * SPAN + (i + 1) * (SPAN // n)] = got.reshape(SPAN // n, TOK, DQ)

    s_sems = {}

    def shared():
        cp_xf.wait()
        for d in range(1, PEERS):
            peer = peer_of(-d)
            recv(SW.at[:, lax.div(peer, NC), :, lax.rem(peer, NC)], sw_sems[d])
        h = dot_nn(XF[...], SW[0].reshape(NX * DQ, HQ))
        a, b = act_grad(h, ssaved[0], ssaved[1])
        for d in list(range(1, NY)) + [0]:
            q = yof(d)
            part = dot_nt(a, SW[1, q].reshape(DQ, HQ)) + dot_nt(b, SW[2, q].reshape(DQ, HQ))
            if d == 0:
                SHO[...] = part
            else:
                SP[d - 1] = part
                s_sems[d] = rsem_new()
                send(SP.at[d - 1], SR.at[d - 1], s_sems[d], ydev(d))

    hidden(0)
    hidden(1)
    activate(1)
    activate(0)
    weigh(1)
    cp_w2.wait()
    for d in range(1, NY):
        recv(W2.at[:, yof(-d)], w2_sems[d])
    keep[3] = outward(1)
    keep[2] = outward(0)
    shared()

    z_sems = {}

    def rs_send(s):
        for direction in range(2):
            off = 9 - s if direction == 0 else s - 9
            cols = pl.ds(direction * (DQ // 2), DQ // 2)
            rs = rsem_new()
            z_sems[(s, direction)] = rs
            dev = zdev(1 if direction == 0 else -1)
            if s == 1:
                ZS[direction, s - 1, :, cols] = PT[slot(off), :, cols].astype(BF)
                send(ZS.at[direction, s - 1, :, cols], ZR.at[direction, s - 1, :, cols], rs, dev)
                continue
            if s == 2:
                recv(ZR.at[direction, 0, :, cols], z_sems[(1, direction)])
                other = pl.ds((1 - direction) * (DQ // 2), DQ // 2)
                ZS[direction, 1, :, cols] = (PT[slot(off), :, cols] + ZR[direction, 0, :, cols].astype(F32)).astype(BF)
                ZS[direction, 1, :, other] = PT[slot(off), :, other].astype(BF)
            else:
                recv(ZR.at[direction, s - 2], z_sems[(s - 1, direction)])
                ZS[direction, s - 1] = (PT[slot(off)] + ZR[direction, s - 2].astype(F32)).astype(BF)
            send(ZS.at[direction, s - 1], ZR.at[direction, s - 1], rs, dev)

    combine(1)
    rs_send(1)
    rs_send(2)
    combine(0)
    for s in range(3, 9):
        rs_send(s)
    total = PT[HOME] + SHO[...]
    for d in range(1, NY):
        recv(SR.at[d - 1], s_sems[d])
        total = total + SR[d - 1]
    for direction in range(2):
        recv(ZR.at[direction, 7], z_sems[(8, direction)])
        total = total + ZR[direction, 7].astype(F32)
    out[...] = total.astype(BF)
    for cp in pending:
        cp.wait_send()


def shards(
    grad_out, expert_ids, gate_values, saved_gate_up, expert_gate_up, expert_down,
    shared_saved, shared_gate_up, shared_down,
):
    meta = jnp.concatenate(
        [expert_ids.T.astype(F32), gate_values.T, jnp.zeros((24 - 2 * TOP, TOK), F32)], axis=0
    )
    sw = jnp.concatenate([shared_down.T[None], shared_gate_up], axis=0)
    anywhere = pl.BlockSpec(memory_space=pl.ANY)
    vmem = pl.BlockSpec(memory_space=pltpu.VMEM)
    slots = NZ * PEERS * CAP
    scratch = [
        pltpu.VMEM((NZ, TOK, DQ), BF),
        pltpu.VMEM((NZ, 24, TOK), F32),
        pltpu.VMEM((3, NX, NZ, NC, 16, HQ), BF),
        pltpu.VMEM((QN * SROWS, SPAN * TOK), BF),
        pltpu.VMEM((GROUPS, SPAN * TOK, QN * SROWS), BF),
        pltpu.VMEM((GROUPS, SPAN * TOK, QN * SROWS), BF),
        pltpu.VMEM((GROUPS, QN, SROWS, DQ), BF),
        pltpu.VMEM((GROUPS, NE, PEERS, SROWS, DQ), BF),
        pltpu.VMEM((NE, NY * HQ, DQ), BF),
        pltpu.VMEM((NE, NY, 2, DQ, HQ), BF),
        pltpu.VMEM((slots, 2 * NE * HQ), BF),
        pltpu.VMEM((GROUPS, ROWS, 2 * NE * HQ), BF),
        pltpu.VMEM((GROUPS, NE, ROWS, HQ), F32),
        pltpu.VMEM((GROUPS, NE, NY - 1, ROWS, HQ), BF),
        pltpu.VMEM((GROUPS, NE, NY - 1, ROWS, HQ), BF),
        pltpu.VMEM((GROUPS, NE, NY, 2, ROWS, HQ), BF),
        pltpu.VMEM((GROUPS, NE, PEERS, SROWS, DQ), BF),
        pltpu.VMEM((GROUPS, QN, SROWS, DQ), BF),
        pltpu.VMEM((NZ, TOK, DQ), F32),
        pltpu.VMEM((2, 8, TOK, DQ), BF),
        pltpu.VMEM((2, 8, TOK, DQ), BF),
        pltpu.VMEM((TOK, NX * DQ), BF),
        pltpu.VMEM((TOK, DQ), F32),
        pltpu.VMEM((NY - 1, TOK, DQ), F32),
        pltpu.VMEM((NY - 1, TOK, DQ), F32),
        pltpu.SemaphoreType.DMA((136,)),
        pltpu.SemaphoreType.DMA((136,)),
        pltpu.SemaphoreType.DMA((16,)),
    ]
    return pl.pallas_call(
        kernel,
        out_shape=jax.ShapeDtypeStruct((TOK, DQ), BF),
        in_specs=[anywhere] * 6 + [vmem],
        out_specs=vmem,
        scratch_shapes=scratch,
        compiler_params=pltpu.CompilerParams(
            collective_id=0, has_side_effects=True, vmem_limit_bytes=60 * 1024 * 1024
        ),
        cost_estimate=pl.CostEstimate(flops=8_000_000_000, bytes_accessed=8_000_000, transcendentals=400_000),
    )(grad_out, meta, sw, saved_gate_up, expert_gate_up, expert_down, shared_saved)


def solution(mesh):
    in_specs = (
        P("ep", None),
        P("ep", None),
        P("ep", None),
        P("ep", None, None, "tp"),
        P("ep", None, None, "tp"),
        P("ep", "tp", None),
        P(None, "ep", "tp"),
        P(None, "ep", "tp"),
        P("tp", "ep"),
    )
    return jax.shard_map(shards, mesh=mesh, in_specs=in_specs, out_specs=P("ep", "tp"), check_vma=False)
```

```python
import functools

import jax
import jax.numpy as jnp
from jax import lax
from jax.experimental import pallas as pl
from jax.experimental.pallas import tpu as pltpu
from jax.sharding import PartitionSpec as P

BF = jnp.bfloat16
F32 = jnp.float32
NX, NZ, NC, NY = 4, 16, 2, 4
PEERS = NX * NC
TOK = 128
CAP = 6
TOP = 10
DQ = 512
HQ = 128
NE = 2
GROUPS = 2
SPAN = NZ // GROUPS
SROWS = SPAN * CAP
QN = PEERS * NE
ROWS = PEERS * SROWS
HOME = 3
AGC = 4
AGR = TOK // AGC
RSC = 4
RSR = TOK // RSC


def dot_nt(a, b):
    return lax.dot_general(a, b, (((1,), (1,)), ((), ())), preferred_element_type=F32)


def dot_nn(a, b):
    return lax.dot_general(a, b, (((1,), (0,)), ((), ())), preferred_element_type=F32)


def dot_tn(a, b):
    return lax.dot_general(a, b, (((0,), (0,)), ((), ())), preferred_element_type=F32)


def act_grad(h, g, u):
    g = g.astype(F32)
    u = u.astype(F32)
    s = jax.nn.sigmoid(g)
    return (h * u * s * (1.0 + g * (1.0 - s))).astype(BF), (h * g * s).astype(BF)


def kernel(
    x_in, ids, gates, sd, sgu, saved, gu, down, ssaved, out,
    XG, MG, SW, SEL, WTH, WTL, SB, R1, W1, W2, SVI, SVP, HO, HS, HR, G, OB, BK, PT, ZS, ZR, XF, SHO, SP, SR,
    ssem, rsem, lsem,
):
    ep = lax.axis_index("ep")
    y = lax.axis_index("tp")
    c = lax.rem(ep, NC)
    z = lax.rem(lax.div(ep, NC), NZ)
    x = lax.div(ep, NC * NZ)
    me = x * NC + c

    def zdev(off):
        return ((x * NZ + lax.rem(z + off + NZ, NZ)) * NC + c, y)

    def pdev(peer):
        return ((lax.div(peer, NC) * NZ + z) * NC + lax.rem(peer, NC), y)

    def peer_of(d):
        return lax.rem(me + d + PEERS, PEERS)

    def yof(d):
        return lax.rem(y + d + NY, NY)

    def ydev(d):
        return (ep, yof(d))

    counts = {"s": 0, "r": 0, "l": 0}
    pending = []

    def rsem_new():
        counts["r"] += 1
        return rsem.at[counts["r"] - 1]

    def send(src, dst, rs, dev):
        ss = ssem.at[counts["s"]]
        counts["s"] += 1
        cp = pltpu.make_async_remote_copy(
            src_ref=src, dst_ref=dst, send_sem=ss, recv_sem=rs, device_id=dev,
            device_id_type=pl.DeviceIdType.MESH,
        )
        cp.start()
        pending.append(cp)

    def recv(dst, rs):
        pltpu.make_async_remote_copy(
            src_ref=dst, dst_ref=dst, send_sem=rs, recv_sem=rs, device_id=(ep, y),
            device_id_type=pl.DeviceIdType.MESH,
        ).wait_recv()

    def local(src, dst):
        cp = pltpu.make_async_copy(src, dst, lsem.at[counts["l"]])
        counts["l"] += 1
        cp.start()
        return cp

    barrier = pltpu.get_barrier_semaphore()
    others = [zdev(1), zdev(-1)] + [pdev(peer_of(d)) for d in range(1, PEERS)] + [ydev(d) for d in range(1, NY)]
    for dev in others:
        pl.semaphore_signal(barrier, inc=1, device_id=dev, device_id_type=pl.DeviceIdType.MESH)
    mine = pl.ds(pl.multiple_of(y * DQ, DQ), DQ)
    cp_x = local(x_in.at[:, mine], XG.at[HOME])
    cp_s = local(sgu, SW.at[pl.ds(1, 2), x, z, c])
    cp_sv = [local(saved.at[e, k], SVI.at[:, pl.ds((2 * e + k) * HQ, HQ)]) for e in range(NE) for k in range(2)]
    cp_w1 = local(down.at[:, :, mine], W1.at[:, pl.ds(pl.multiple_of(y * HQ, HQ), HQ), :])
    cp_w2 = local(gu.at[:, :, mine, :], W2.at[:, y])
    cp_xf = local(x_in, XF)
    pl.semaphore_wait(barrier, len(others))

    def slot(off):
        return (off + HOME) % NZ

    ag_sems = {}
    SWI = AGC + 1

    def ag_ref(s, direction, i):
        off = -s if direction == 0 else s
        k = slot(off)
        if s == 8 and (i in (0, SWI) or 1 <= i <= AGC // 2) != (direction == 0):
            return None
        if i == 0:
            return MG.at[k]
        if i == SWI:
            return SW.at[:, x, lax.rem(z + off + NZ, NZ), c]
        return XG.at[k, pl.ds((i - 1) * AGR, AGR), :]

    def ag_send(s, direction, i):
        there = ag_ref(s, direction, i)
        if there is None:
            return
        off = -s if direction == 0 else s
        k = slot(off)
        src = ag_ref(s - 1, direction, i) if s < 9 else None
        if i == 0:
            dst = MG.at[k]
        elif i == SWI:
            dst = src
        else:
            dst = XG.at[k, pl.ds((i - 1) * AGR, AGR), :]
            if s == 1:
                src = x_in.at[pl.ds((i - 1) * AGR, AGR), mine]
        rs = rsem_new()
        ag_sems[(s, direction, i)] = rs
        send(src, dst, rs, zdev(1 if direction == 0 else -1))

    for i in range(1, AGC + 1):
        for direction in range(2):
            ag_send(1, direction, i)

    MG[HOME, 0:TOP] = ids[...].astype(F32)
    MG[HOME, TOP:2 * TOP] = gates[...]
    MG[HOME, 2 * TOP:24] = jnp.zeros((24 - 2 * TOP, TOK), F32)
    SW[0, x, z, c] = sd[...]
    for direction in range(2):
        ag_send(1, direction, 0)
    cp_s.wait()
    for direction in range(2):
        ag_send(1, direction, SWI)

    w1_sems, w2_sems = {}, {}
    for d in range(1, NY):
        w1_sems[d] = rsem_new()
        there = pl.ds(pl.multiple_of(yof(d) * DQ, DQ), DQ)
        send(down.at[:, :, there], W1.at[:, pl.ds(pl.multiple_of(y * HQ, HQ), HQ), :], w1_sems[d], ydev(d))
    for d in range(1, NY):
        w2_sems[d] = rsem_new()
        there = pl.ds(pl.multiple_of(yof(d) * DQ, DQ), DQ)
        send(gu.at[:, :, there, :], W2.at[:, y], w2_sems[d], ydev(d))

    for cp in cp_sv:
        cp.wait()

    def permute_saved(g):
        shape = (PEERS, SROWS, NZ * PEERS * CAP)
        src = lax.broadcasted_iota(jnp.int32, shape, 0)
        i = lax.broadcasted_iota(jnp.int32, shape, 1)
        lane = lax.broadcasted_iota(jnp.int32, shape, 2)
        j = lax.shift_right_logical(i * 43, 8)
        zz = (z + j + (SPAN * g - HOME + NZ)) & (NZ - 1)
        target = lax.shift_right_logical(src, 1) * (NZ * NC * CAP) + zz * (NC * CAP) + (src & 1) * CAP + (i - j * CAP)
        pick = jnp.where(target == lane, 1.0, 0.0).astype(BF).reshape(ROWS, NZ * PEERS * CAP)
        SVP[g] = dot_nn(pick, SVI[...]).astype(BF)

    qi = lax.broadcasted_iota(jnp.int32, (QN, TOK), 0)
    expert = (lax.shift_right_logical(qi, 2) * (NZ * NC * NE) + z * (NC * NE) + (qi & 3)).astype(F32)
    before = jnp.where(
        lax.broadcasted_iota(jnp.int32, (TOK, TOK), 0) < lax.broadcasted_iota(jnp.int32, (TOK, TOK), 1), 1.0, 0.0
    ).astype(BF)
    row3 = lax.broadcasted_iota(jnp.int32, (QN, SROWS, TOK), 1).astype(F32)
    lane_q = lax.broadcasted_iota(jnp.int32, (QN, QN * SROWS), 1)
    row_q = lax.broadcasted_iota(jnp.int32, (QN, QN * SROWS), 0)
    in_q = (lane_q >= row_q * SROWS) & (lane_q < row_q * SROWS + SROWS)
    spread = jnp.where(in_q, 1.0, 0.0).astype(BF)
    lane_i = jnp.sum(jnp.where(in_q, lane_q - row_q * SROWS, 0).astype(F32), axis=0, keepdims=True)

    def place(k):
        meta = MG[k]
        named = jnp.zeros((QN, TOK), F32)
        gate = jnp.zeros((QN, TOK), F32)
        for i in range(TOP):
            hit = meta[i:i + 1, :] == expert
            named = jnp.where(hit, 1.0, named)
            gate = jnp.where(hit, meta[TOP + i:TOP + i + 1, :], gate)
        rank = dot_nn(named.astype(BF), before)
        key = jnp.where(named > 0.5, rank + float((k % SPAN) * CAP), -1.0)
        return key, gate

    x_sems, b_sems = {}, {}

    def select(g):
        for j in range(SPAN):
            key, gate = place(g * SPAN + j)
            hot = jnp.where(key[:, None, :] == row3, 1.0, 0.0).astype(BF)
            SEL[:, pl.ds(j * TOK, TOK)] = hot.reshape(QN * SROWS, TOK)
        rows = XG[g * SPAN:(g + 1) * SPAN].reshape(SPAN * TOK, DQ)
        half = QN * SROWS // 2
        for h in range(2):
            got = dot_nn(SEL[pl.ds(h * half, half), :], rows).astype(BF)
            SB[g, h * (QN // 2):(h + 1) * (QN // 2)] = got.reshape(QN // 2, SROWS, DQ)
        for d in range(1, PEERS):
            rs = rsem_new()
            x_sems[(g, d)] = rs
            peer = peer_of(d)
            send(SB.at[g, pl.ds(peer * NE, NE)], R1.at[g, :, me], rs, pdev(peer))
        return local(SB.at[g, pl.ds(me * NE, NE)], R1.at[g, :, me])

    def weigh(g):
        for j in range(SPAN):
            key, gate = place(g * SPAN + j)
            high = gate.astype(BF)
            low = (gate - high.astype(F32)).astype(BF)
            where = dot_tn(key.astype(BF), spread) == lane_i
            at = pl.ds(j * TOK, TOK)
            WTH[g, at, :] = jnp.where(where, dot_tn(high, spread), 0.0).astype(BF)
            WTL[g, at, :] = jnp.where(where, dot_tn(low, spread), 0.0).astype(BF)

    keep = {}
    cp_x.wait()
    for s in range(1, 9):
        for i in range(AGC + 2):
            for direction in range(2):
                ref = ag_ref(s, direction, i)
                if ref is None:
                    continue
                recv(ref, ag_sems[(s, direction, i)])
                if s < 8:
                    ag_send(s + 1, direction, i)
        if s == 1:
            permute_saved(0)
        if s == 2:
            permute_saved(1)
        if s == 4:
            keep[0] = select(0)
        if s == 5:
            weigh(0)

    sw_sems = {}
    keep[1] = select(1)

    def spread_shared():
        for d in range(1, PEERS):
            sw_sems[d] = rsem_new()
            part = SW.at[:, x, :, c]
            send(part, part, sw_sems[d], pdev(peer_of(d)))

    h_sems, g_sems = {}, {}
    cp_w1.wait()
    for d in range(1, NY):
        src = yof(-d)
        recv(W1.at[:, pl.ds(pl.multiple_of(src * HQ, HQ), HQ), :], w1_sems[d])

    def hidden(g):
        keep[g].wait()
        for d in range(1, PEERS):
            recv(R1.at[g, :, peer_of(-d)], x_sems[(g, d)])
        for e in range(NE):
            rows = R1[g, e].reshape(ROWS, DQ)
            for d in list(range(1, NY)) + [0]:
                q = yof(d)
                part = dot_nt(rows, W1[e, pl.ds(pl.multiple_of(q * HQ, HQ), HQ), :])
                if d == 0:
                    HO[g, e] = part
                else:
                    HS[g, e, d - 1] = part.astype(BF)
                    rs = rsem_new()
                    h_sems[(g, e, d)] = rs
                    send(HS.at[g, e, d - 1], HR.at[g, e, d - 1], rs, ydev(d))

    def activate(g, e):
        h = HO[g, e]
        for d in range(1, NY):
            recv(HR.at[g, e, d - 1], h_sems[(g, e, d)])
            h = h + HR[g, e, d - 1].astype(F32)
        gate_pre = SVP[g, :, pl.ds(2 * e * HQ, HQ)]
        up_pre = SVP[g, :, pl.ds((2 * e + 1) * HQ, HQ)]
        a, b = act_grad(h, gate_pre, up_pre)
        G[g, e, y, 0] = a
        G[g, e, y, 1] = b
        for d in (1, -1):
            rs = rsem_new()
            g_sems[(g, e, d)] = rs
            send(G.at[g, e, y], G.at[g, e, y], rs, ydev(d))

    def relay(g, e):
        for k, d in ((0, 1), (1, -1)):
            piece = G.at[g, e, yof(-d)]
            recv(piece, g_sems[(g, e, d)])
            rs = rsem_new()
            g_sems[(g, e, 2, k)] = rs
            send(piece.at[k], piece.at[k], rs, ydev(d))

    def outward(g):
        for e in range(NE):
            for k in range(2):
                recv(G.at[g, e, yof(2), k], g_sems[(g, e, 2, k)])
            left = jnp.concatenate([G[g, e, q, k] for q in range(NY) for k in range(2)], axis=1)
            right = jnp.concatenate([W2[e, q, k] for q in range(NY) for k in range(2)], axis=1)
            OB[g, e] = dot_nt(left, right).astype(BF).reshape(PEERS, SROWS, DQ)
        for d in range(1, PEERS):
            rs = rsem_new()
            b_sems[(g, d)] = rs
            peer = peer_of(d)
            send(OB.at[g, :, peer], BK.at[g, pl.ds(me * NE, NE)], rs, pdev(peer))
        return local(OB.at[g, :, me], BK.at[g, pl.ds(me * NE, NE)])

    def combine(g):
        keep[g + 2].wait()
        for d in range(1, PEERS):
            recv(BK.at[g, pl.ds(peer_of(-d) * NE, NE)], b_sems[(g, d)])
        rows = BK[g].reshape(QN * SROWS, DQ)
        n = 4
        size = SPAN * TOK // n
        for i in range(n):
            at = pl.ds(i * size, size)
            got = dot_nn(WTH[g, at, :], rows) + dot_nn(WTL[g, at, :], rows)
            PT[g * SPAN + i * (SPAN // n):g * SPAN + (i + 1) * (SPAN // n)] = got.reshape(SPAN // n, TOK, DQ)

    s_sems = {}

    def shared_products():
        cp_xf.wait()
        for d in range(1, PEERS):
            peer = peer_of(-d)
            recv(SW.at[:, lax.div(peer, NC), :, lax.rem(peer, NC)], sw_sems[d])
        h = dot_nn(XF[...], SW[0].reshape(NX * DQ, HQ))
        a, b = act_grad(h, ssaved[0], ssaved[1])
        for d in list(range(1, NY)) + [0]:
            q = yof(d)
            part = dot_nt(a, SW[1, q].reshape(DQ, HQ)) + dot_nt(b, SW[2, q].reshape(DQ, HQ))
            if d == 0:
                SHO[...] = part
            else:
                SP[d - 1] = part

    def shared_sum():
        for d in range(1, NY):
            s_sems[d] = rsem_new()
            send(SP.at[d - 1], SR.at[d - 1], s_sems[d], ydev(d))

    hidden(0)
    weigh(1)
    activate(0, 0)
    hidden(1)
    spread_shared()
    activate(1, 0)
    activate(1, 1)
    relay(0, 0)
    activate(0, 1)
    relay(1, 0)
    relay(1, 1)
    cp_w2.wait()
    for d in range(1, NY):
        recv(W2.at[:, yof(-d)], w2_sems[d])
    keep[3] = outward(1)
    relay(0, 1)
    shared_products()
    keep[2] = outward(0)
    shared_sum()

    z_sems = {}

    def rs_step(s):
        for i in range(RSC):
            rows = pl.ds(i * RSR, RSR)
            for direction in range(2):
                if s == 1 and (i < RSC // 2) != (direction == 0):
                    continue
                off = 9 - s if direction == 0 else s - 9
                part = PT[slot(off), rows, :]
                if (s - 1, direction, i) in z_sems:
                    recv(ZR.at[direction, s - 2, rows, :], z_sems[(s - 1, direction, i)])
                    part = part + ZR[direction, s - 2, rows, :].astype(F32)
                ZS[direction, s - 1, rows, :] = part.astype(BF)
                rs = rsem_new()
                z_sems[(s, direction, i)] = rs
                send(
                    ZS.at[direction, s - 1, rows, :], ZR.at[direction, s - 1, rows, :], rs,
                    zdev(1 if direction == 0 else -1),
                )

    combine(1)
    rs_step(1)
    rs_step(2)
    rs_step(3)
    combine(0)
    for s in range(4, 9):
        rs_step(s)
    total = PT[HOME] + SHO[...]
    for d in range(1, NY):
        recv(SR.at[d - 1], s_sems[d])
        total = total + SR[d - 1]
    PT[HOME] = total
    for i in range(RSC):
        rows = pl.ds(i * RSR, RSR)
        part = PT[HOME, rows, :]
        for direction in range(2):
            recv(ZR.at[direction, 7, rows, :], z_sems[(8, direction, i)])
            part = part + ZR[direction, 7, rows, :].astype(F32)
        out[rows, :] = part.astype(BF)
    for cp in pending:
        cp.wait_send()


def shards(
    grad_out, expert_ids, gate_values, saved_gate_up, expert_gate_up, expert_down,
    shared_saved, shared_gate_up, shared_down,
):
    anywhere = pl.BlockSpec(memory_space=pl.ANY)
    vmem = pl.BlockSpec(memory_space=pltpu.VMEM)
    slots = NZ * PEERS * CAP
    scratch = [
        pltpu.VMEM((NZ, TOK, DQ), BF),
        pltpu.VMEM((NZ, 24, TOK), F32),
        pltpu.VMEM((3, NX, NZ, NC, 16, HQ), BF),
        pltpu.VMEM((QN * SROWS, SPAN * TOK), BF),
        pltpu.VMEM((GROUPS, SPAN * TOK, QN * SROWS), BF),
        pltpu.VMEM((GROUPS, SPAN * TOK, QN * SROWS), BF),
        pltpu.VMEM((GROUPS, QN, SROWS, DQ), BF),
        pltpu.VMEM((GROUPS, NE, PEERS, SROWS, DQ), BF),
        pltpu.VMEM((NE, NY * HQ, DQ), BF),
        pltpu.VMEM((NE, NY, 2, DQ, HQ), BF),
        pltpu.VMEM((slots, 2 * NE * HQ), BF),
        pltpu.VMEM((GROUPS, ROWS, 2 * NE * HQ), BF),
        pltpu.VMEM((GROUPS, NE, ROWS, HQ), F32),
        pltpu.VMEM((GROUPS, NE, NY - 1, ROWS, HQ), BF),
        pltpu.VMEM((GROUPS, NE, NY - 1, ROWS, HQ), BF),
        pltpu.VMEM((GROUPS, NE, NY, 2, ROWS, HQ), BF),
        pltpu.VMEM((GROUPS, NE, PEERS, SROWS, DQ), BF),
        pltpu.VMEM((GROUPS, QN, SROWS, DQ), BF),
        pltpu.VMEM((NZ, TOK, DQ), F32),
        pltpu.VMEM((2, 8, TOK, DQ), BF),
        pltpu.VMEM((2, 8, TOK, DQ), BF),
        pltpu.VMEM((TOK, NX * DQ), BF),
        pltpu.VMEM((TOK, DQ), F32),
        pltpu.VMEM((NY - 1, TOK, DQ), F32),
        pltpu.VMEM((NY - 1, TOK, DQ), F32),
        pltpu.SemaphoreType.DMA((228,)),
        pltpu.SemaphoreType.DMA((228,)),
        pltpu.SemaphoreType.DMA((16,)),
    ]
    return pl.pallas_call(
        kernel,
        out_shape=jax.ShapeDtypeStruct((TOK, DQ), BF),
        in_specs=[anywhere, vmem, vmem, vmem, anywhere, anywhere, anywhere, anywhere, vmem],
        out_specs=vmem,
        scratch_shapes=scratch,
        compiler_params=pltpu.CompilerParams(
            collective_id=0, has_side_effects=True, vmem_limit_bytes=60 * 1024 * 1024
        ),
        cost_estimate=pl.CostEstimate(flops=8_000_000_000, bytes_accessed=8_000_000, transcendentals=400_000),
    )(
        grad_out, expert_ids.T, gate_values.T, shared_down.T, shared_gate_up, saved_gate_up, expert_gate_up, expert_down,
        shared_saved,
    )


def solution(mesh):
    in_specs = (
        P("ep", None),
        P("ep", None),
        P("ep", None),
        P("ep", None, None, "tp"),
        P("ep", None, None, "tp"),
        P("ep", "tp", None),
        P(None, "ep", "tp"),
        P(None, "ep", "tp"),
        P("tp", "ep"),
    )
    return jax.shard_map(shards, mesh=mesh, in_specs=in_specs, out_specs=P("ep", "tp"), check_vma=False)
```

```python
import functools

import jax
import jax.numpy as jnp
from jax import lax
from jax.experimental import pallas as pl
from jax.experimental.pallas import tpu as pltpu
from jax.sharding import PartitionSpec as P

BF = jnp.bfloat16
F32 = jnp.float32
NX, NZ, NC, NY = 4, 16, 2, 4
PEERS = NX * NC
TOK = 128
CAP = 6
TOP = 10
DQ = 512
HQ = 128
NE = 2
GROUPS = 4
SPAN = NZ // GROUPS
SROWS = SPAN * CAP
QN = PEERS * NE
PR = NE * SROWS
ROWS = PEERS * PR
HOME = 0
AGC = 4
AGR = TOK // AGC
RSC = 4
RSR = TOK // RSC
OFFS = (0, 1, -1, 2, -2, 3, -3, 4, -4, 5, -5, 6, -6, 7, -7, 8)


def dot_nt(a, b):
    return lax.dot_general(a, b, (((1,), (1,)), ((), ())), preferred_element_type=F32)


def dot_nn(a, b):
    return lax.dot_general(a, b, (((1,), (0,)), ((), ())), preferred_element_type=F32)


def dot_tn(a, b):
    return lax.dot_general(a, b, (((0,), (0,)), ((), ())), preferred_element_type=F32)


def act_grad(h, g, u):
    g = g.astype(F32)
    u = u.astype(F32)
    s = jax.nn.sigmoid(g)
    return (h * u * s * (1.0 + g * (1.0 - s))).astype(BF), (h * g * s).astype(BF)


def kernel(
    x_in, ids, gates, sd, sgu, saved, gu, down, ssaved, out,
    XG, MG, SW, SEL, WTH, WTL, SB, R1, W1, W2, SVI, SVP, HO, HS, HR, G, OB, BK, PT, ZS, ZR, XF, SHO, SP, SR,
    ssem, rsem, lsem,
):
    ep = lax.axis_index("ep")
    y = lax.axis_index("tp")
    c = lax.rem(ep, NC)
    z = lax.rem(lax.div(ep, NC), NZ)
    x = lax.div(ep, NC * NZ)
    me = x * NC + c

    def zdev(off):
        return ((x * NZ + lax.rem(z + off + NZ, NZ)) * NC + c, y)

    def pdev(peer):
        return ((lax.div(peer, NC) * NZ + z) * NC + lax.rem(peer, NC), y)

    def peer_of(d):
        return lax.rem(me + d + PEERS, PEERS)

    def yof(d):
        return lax.rem(y + d + NY, NY)

    def ydev(d):
        return (ep, yof(d))

    counts = {"s": 0, "r": 0, "l": 0}
    pending = []

    def rsem_new():
        counts["r"] += 1
        return rsem.at[counts["r"] - 1]

    def send(src, dst, rs, dev):
        ss = ssem.at[counts["s"]]
        counts["s"] += 1
        cp = pltpu.make_async_remote_copy(
            src_ref=src, dst_ref=dst, send_sem=ss, recv_sem=rs, device_id=dev,
            device_id_type=pl.DeviceIdType.MESH,
        )
        cp.start()
        pending.append(cp)

    def recv(dst, rs):
        pltpu.make_async_remote_copy(
            src_ref=dst, dst_ref=dst, send_sem=rs, recv_sem=rs, device_id=(ep, y),
            device_id_type=pl.DeviceIdType.MESH,
        ).wait_recv()

    def local(src, dst):
        cp = pltpu.make_async_copy(src, dst, lsem.at[counts["l"]])
        counts["l"] += 1
        cp.start()
        return cp

    barrier = pltpu.get_barrier_semaphore()
    others = [zdev(1), zdev(-1)] + [pdev(peer_of(d)) for d in range(1, PEERS)] + [ydev(d) for d in range(1, NY)]
    for dev in others:
        pl.semaphore_signal(barrier, inc=1, device_id=dev, device_id_type=pl.DeviceIdType.MESH)
    mine = pl.ds(pl.multiple_of(y * DQ, DQ), DQ)
    cp_x = local(x_in.at[:, mine], XG.at[HOME])
    cp_s = local(sgu, SW.at[pl.ds(1, 2), x, z, c])
    cp_sv = [local(saved.at[e, k], SVI.at[:, pl.ds((2 * e + k) * HQ, HQ)]) for e in range(NE) for k in range(2)]
    cp_w1 = local(down.at[:, :, mine], W1.at[:, pl.ds(pl.multiple_of(y * HQ, HQ), HQ), :])
    cp_w2 = local(gu.at[:, :, mine, :], W2.at[:, y])
    cp_xf = local(x_in, XF)
    pl.semaphore_wait(barrier, len(others))

    def slot(off):
        return OFFS.index(8 if off == -8 else off)

    ag_sems = {}
    SWI = AGC + 1

    def ag_ref(s, direction, i):
        off = -s if direction == 0 else s
        k = slot(off)
        if s == 8 and (i in (0, SWI) or 1 <= i <= AGC // 2) != (direction == 0):
            return None
        if i == 0:
            return MG.at[k]
        if i == SWI:
            return SW.at[:, x, lax.rem(z + off + NZ, NZ), c]
        return XG.at[k, pl.ds((i - 1) * AGR, AGR), :]

    def ag_send(s, direction, i):
        there = ag_ref(s, direction, i)
        if there is None:
            return
        off = -s if direction == 0 else s
        k = slot(off)
        src = ag_ref(s - 1, direction, i) if s < 9 else None
        if i == 0:
            dst = MG.at[k]
        elif i == SWI:
            dst = src
        else:
            dst = XG.at[k, pl.ds((i - 1) * AGR, AGR), :]
            if s == 1:
                src = x_in.at[pl.ds((i - 1) * AGR, AGR), mine]
        rs = rsem_new()
        ag_sems[(s, direction, i)] = rs
        send(src, dst, rs, zdev(1 if direction == 0 else -1))

    MG[HOME, 0:TOP] = ids[...].astype(F32)
    MG[HOME, TOP:2 * TOP] = gates[...]
    MG[HOME, 2 * TOP:24] = jnp.zeros((24 - 2 * TOP, TOK), F32)
    SW[0, x, z, c] = sd[...]
    w1_sems, w2_sems = {}, {}

    def send_w1():
        for d in range(1, NY):
            w1_sems[d] = rsem_new()
            there = pl.ds(pl.multiple_of(yof(d) * DQ, DQ), DQ)
            send(down.at[:, :, there], W1.at[:, pl.ds(pl.multiple_of(y * HQ, HQ), HQ), :], w1_sems[d], ydev(d))

    def send_w2():
        for d in range(1, NY):
            w2_sems[d] = rsem_new()
            there = pl.ds(pl.multiple_of(yof(d) * DQ, DQ), DQ)
            send(gu.at[:, :, there, :], W2.at[:, y], w2_sems[d], ydev(d))

    for direction in range(2):
        ag_send(1, direction, 0)
    send_w1()
    for i in range(1, AGC + 1):
        for direction in range(2):
            ag_send(1, direction, i)
    cp_s.wait()
    for direction in range(2):
        ag_send(1, direction, SWI)

    for cp in cp_sv:
        cp.wait()

    def second(width):
        return lax.broadcasted_iota(jnp.int32, (PEERS, PR, width), 1).reshape(ROWS, width) >= SROWS

    def permute_saved(g):
        shape = (PEERS, PR, NZ * PEERS * CAP)
        src = lax.broadcasted_iota(jnp.int32, shape, 0)
        i = lax.broadcasted_iota(jnp.int32, shape, 1)
        lane = lax.broadcasted_iota(jnp.int32, shape, 2)
        i = jnp.where(i >= SROWS, i - SROWS, i)
        j = lax.shift_right_logical(i * 43, 8)
        offs = [(o + NZ) % NZ for o in OFFS[g * SPAN:(g + 1) * SPAN]]
        off = jnp.where(j == 0, offs[0], jnp.where(j == 1, offs[1], jnp.where(j == 2, offs[2], offs[3])))
        zz = (z + off) & (NZ - 1)
        target = lax.shift_right_logical(src, 1) * (NZ * NC * CAP) + zz * (NC * CAP) + (src & 1) * CAP + (i - j * CAP)
        pick = jnp.where(target == lane, 1.0, 0.0).astype(BF).reshape(ROWS, NZ * PEERS * CAP)
        got = dot_nn(pick, SVI[...])
        SVP[g] = jnp.where(second(2 * HQ), got[:, 2 * HQ:], got[:, :2 * HQ]).astype(BF)

    qi = lax.broadcasted_iota(jnp.int32, (QN, TOK), 0)
    expert = (lax.shift_right_logical(qi, 2) * (NZ * NC * NE) + z * (NC * NE) + (qi & 3)).astype(F32)
    before = jnp.where(
        lax.broadcasted_iota(jnp.int32, (TOK, TOK), 0) < lax.broadcasted_iota(jnp.int32, (TOK, TOK), 1), 1.0, 0.0
    ).astype(BF)
    row3 = lax.broadcasted_iota(jnp.int32, (QN, SROWS, TOK), 1).astype(F32)
    lane_q = lax.broadcasted_iota(jnp.int32, (QN, QN * SROWS), 1)
    row_q = lax.broadcasted_iota(jnp.int32, (QN, QN * SROWS), 0)
    in_q = (lane_q >= row_q * SROWS) & (lane_q < row_q * SROWS + SROWS)
    spread = jnp.where(in_q, 1.0, 0.0).astype(BF)
    lane_i = jnp.sum(jnp.where(in_q, lane_q - row_q * SROWS, 0).astype(F32), axis=0, keepdims=True)

    def place(k):
        meta = MG[k]
        named = jnp.zeros((QN, TOK), F32)
        gate = jnp.zeros((QN, TOK), F32)
        for i in range(TOP):
            hit = meta[i:i + 1, :] == expert
            named = jnp.where(hit, 1.0, named)
            gate = jnp.where(hit, meta[TOP + i:TOP + i + 1, :], gate)
        rank = dot_nn(named.astype(BF), before)
        key = jnp.where(named > 0.5, rank + float((k % SPAN) * CAP), -1.0)
        return key, gate

    x_sems, b_sems = {}, {}

    def select(g):
        for j in range(SPAN):
            key, gate = place(g * SPAN + j)
            hot = jnp.where(key[:, None, :] == row3, 1.0, 0.0).reshape(QN * SROWS, TOK)
            SEL[:, pl.ds(j * TOK, TOK)] = hot.astype(BF)
        rows = XG[g * SPAN:(g + 1) * SPAN].reshape(SPAN * TOK, DQ)
        SB[g] = dot_nn(SEL[...], rows).astype(BF).reshape(PEERS, PR, DQ)
        for d in range(1, PEERS):
            rs = rsem_new()
            x_sems[(g, d)] = rs
            peer = peer_of(d)
            send(SB.at[g, peer], R1.at[g, me], rs, pdev(peer))
        return local(SB.at[g, me], R1.at[g, me])

    def weigh(g):
        for j in range(SPAN):
            key, gate = place(g * SPAN + j)
            high = gate.astype(BF)
            low = (gate - high.astype(F32)).astype(BF)
            where = dot_tn(key.astype(BF), spread) == lane_i
            at = pl.ds(j * TOK, TOK)
            WTH[g, at, :] = jnp.where(where, dot_tn(high, spread), 0.0).astype(BF)
            WTL[g, at, :] = jnp.where(where, dot_tn(low, spread), 0.0).astype(BF)

    keep, sw_sems, h_sems, g_sems = {}, {}, {}, {}

    def spread_shared():
        for d in range(1, PEERS):
            sw_sems[d] = rsem_new()
            part = SW.at[:, x, :, c]
            send(part, part, sw_sems[d], pdev(peer_of(d)))

    def wait_w1():
        cp_w1.wait()
        for d in range(1, NY):
            recv(W1.at[:, pl.ds(pl.multiple_of(yof(-d) * HQ, HQ), HQ), :], w1_sems[d])

    def wait_w2():
        cp_w2.wait()
        for d in range(1, NY):
            recv(W2.at[:, yof(-d)], w2_sems[d])

    def hidden(g):
        keep[g].wait()
        for d in range(1, PEERS):
            recv(R1.at[g, peer_of(-d)], x_sems[(g, d)])
        rows = R1[g].reshape(ROWS, DQ)
        mine_second = second(HQ)
        for d in (1, 2, 3, 0):
            quarter = pl.ds(pl.multiple_of(yof(d) * HQ, HQ), HQ)
            both = dot_nt(rows, jnp.concatenate([W1[e, quarter, :] for e in range(NE)], axis=0))
            part = jnp.where(mine_second, both[:, HQ:], both[:, :HQ])
            if d == 0:
                HO[g] = part
            else:
                HS[g, d - 1] = part.astype(BF)
                rs = rsem_new()
                h_sems[(g, d)] = rs
                send(HS.at[g, d - 1], HR.at[g, d - 1], rs, ydev(d))

    def activate(g):
        h = HO[g]
        for d in range(1, NY):
            recv(HR.at[g, d - 1], h_sems[(g, d)])
            h = h + HR[g, d - 1].astype(F32)
        a, b = act_grad(h, SVP[g, :, pl.ds(0, HQ)], SVP[g, :, pl.ds(HQ, HQ)])
        G[g, y, 0] = a
        G[g, y, 1] = b
        for d in (1, -1):
            rs = rsem_new()
            g_sems[(g, d)] = rs
            send(G.at[g, y], G.at[g, y], rs, ydev(d))

    def relay(g):
        for k, d in ((0, 1), (1, -1)):
            piece = G.at[g, yof(-d)]
            recv(piece, g_sems[(g, d)])
            rs = rsem_new()
            g_sems[(g, 2, k)] = rs
            send(piece.at[k], piece.at[k], rs, ydev(d))

    def outward(g):
        for k in range(2):
            recv(G.at[g, yof(2), k], g_sems[(g, 2, k)])
        left = jnp.concatenate([G[g, q, k] for q in range(NY) for k in range(2)], axis=1)
        parts = []
        for e in range(NE):
            right = jnp.concatenate([W2[e, q, k] for q in range(NY) for k in range(2)], axis=1)
            parts.append(dot_nt(left, right))
        OB[g] = jnp.where(second(DQ), parts[1], parts[0]).astype(BF).reshape(PEERS, PR, DQ)
        for d in range(1, PEERS):
            rs = rsem_new()
            b_sems[(g, d)] = rs
            peer = peer_of(d)
            send(OB.at[g, peer], BK.at[g, me], rs, pdev(peer))
        keep[g + GROUPS] = local(OB.at[g, me], BK.at[g, me])

    def combine(g):
        keep[g + GROUPS].wait()
        for d in range(1, PEERS):
            recv(BK.at[g, peer_of(-d)], b_sems[(g, d)])
        rows = BK[g].reshape(ROWS, DQ)
        got = dot_nn(WTH[g], rows) + dot_nn(WTL[g], rows)
        PT[g * SPAN:(g + 1) * SPAN] = got.reshape(SPAN, TOK, DQ)

    s_sems = {}

    def shared_products():
        cp_xf.wait()
        for d in range(1, PEERS):
            peer = peer_of(-d)
            recv(SW.at[:, lax.div(peer, NC), :, lax.rem(peer, NC)], sw_sems[d])
        h = dot_nn(XF[...], SW[0].reshape(NX * DQ, HQ))
        a, b = act_grad(h, ssaved[0], ssaved[1])
        for d in list(range(1, NY)) + [0]:
            q = yof(d)
            part = dot_nt(a, SW[1, q].reshape(DQ, HQ)) + dot_nt(b, SW[2, q].reshape(DQ, HQ))
            if d == 0:
                SHO[...] = part
            else:
                SP[d - 1] = part.astype(BF)

    def shared_sum():
        for d in range(1, NY):
            s_sems[d] = rsem_new()
            send(SP.at[d - 1], SR.at[d - 1], s_sems[d], ydev(d))

    z_sems = {}

    def rs_step(s):
        for i in range(RSC):
            rows = pl.ds(i * RSR, RSR)
            for direction in range(2):
                if s == 1 and (i < RSC // 2) != (direction == 0):
                    continue
                off = 9 - s if direction == 0 else s - 9
                part = PT[slot(off), rows, :]
                if (s - 1, direction, i) in z_sems:
                    recv(ZR.at[direction, s - 2, rows, :], z_sems[(s - 1, direction, i)])
                    part = part + ZR[direction, s - 2, rows, :].astype(F32)
                ZS[direction, s - 1, rows, :] = part.astype(BF)
                rs = rsem_new()
                z_sems[(s, direction, i)] = rs
                send(
                    ZS.at[direction, s - 1, rows, :], ZR.at[direction, s - 1, rows, :], rs,
                    zdev(1 if direction == 0 else -1),
                )

    cp_x.wait()
    for s in range(1, 9):
        for i in range(AGC + 2):
            for direction in range(2):
                ref = ag_ref(s, direction, i)
                if ref is None:
                    continue
                recv(ref, ag_sems[(s, direction, i)])
                if s < 8:
                    ag_send(s + 1, direction, i)
        if s == 1:
            permute_saved(0)
        if s == 2:
            keep[0] = select(0)
            send_w2()
        if s == 3:
            permute_saved(1)
        if s == 4:
            keep[1] = select(1)
        if s == 5:
            wait_w1()
            hidden(0)
        if s == 6:
            keep[2] = select(2)
        if s == 7:
            hidden(1)
    keep[3] = select(3)
    hidden(2)
    permute_saved(3)
    weigh(3)
    hidden(3)
    spread_shared()
    permute_saved(2)
    activate(3)
    weigh(2)
    weigh(1)
    relay(3)
    activate(2)
    wait_w2()
    outward(3)
    relay(2)
    activate(1)
    weigh(0)
    shared_products()
    combine(3)
    rs_step(1)
    outward(2)
    relay(1)
    activate(0)
    shared_sum()
    rs_step(2)
    combine(2)
    rs_step(3)
    outward(1)
    relay(0)
    rs_step(4)
    combine(1)
    rs_step(5)
    outward(0)
    rs_step(6)
    combine(0)
    rs_step(7)
    rs_step(8)
    total = PT[HOME] + SHO[...]
    for d in range(1, NY):
        recv(SR.at[d - 1], s_sems[d])
        total = total + SR[d - 1].astype(F32)
    PT[HOME] = total
    for i in range(RSC):
        rows = pl.ds(i * RSR, RSR)
        part = PT[HOME, rows, :]
        for direction in range(2):
            recv(ZR.at[direction, 7, rows, :], z_sems[(8, direction, i)])
            part = part + ZR[direction, 7, rows, :].astype(F32)
        out[rows, :] = part.astype(BF)
    for cp in pending:
        cp.wait_send()


def shards(
    grad_out, expert_ids, gate_values, saved_gate_up, expert_gate_up, expert_down,
    shared_saved, shared_gate_up, shared_down,
):
    anywhere = pl.BlockSpec(memory_space=pl.ANY)
    vmem = pl.BlockSpec(memory_space=pltpu.VMEM)
    slots = NZ * PEERS * CAP
    scratch = [
        pltpu.VMEM((NZ, TOK, DQ), BF),
        pltpu.VMEM((NZ, 24, TOK), F32),
        pltpu.VMEM((3, NX, NZ, NC, 16, HQ), BF),
        pltpu.VMEM((ROWS, SPAN * TOK), BF),
        pltpu.VMEM((GROUPS, SPAN * TOK, ROWS), BF),
        pltpu.VMEM((GROUPS, SPAN * TOK, ROWS), BF),
        pltpu.VMEM((GROUPS, PEERS, PR, DQ), BF),
        pltpu.VMEM((GROUPS, PEERS, PR, DQ), BF),
        pltpu.VMEM((NE, NY * HQ, DQ), BF),
        pltpu.VMEM((NE, NY, 2, DQ, HQ), BF),
        pltpu.VMEM((slots, 2 * NE * HQ), BF),
        pltpu.VMEM((GROUPS, ROWS, 2 * HQ), BF),
        pltpu.VMEM((GROUPS, ROWS, HQ), F32),
        pltpu.VMEM((GROUPS, NY - 1, ROWS, HQ), BF),
        pltpu.VMEM((GROUPS, NY - 1, ROWS, HQ), BF),
        pltpu.VMEM((GROUPS, NY, 2, ROWS, HQ), BF),
        pltpu.VMEM((GROUPS, PEERS, PR, DQ), BF),
        pltpu.VMEM((GROUPS, PEERS, PR, DQ), BF),
        pltpu.VMEM((NZ, TOK, DQ), F32),
        pltpu.VMEM((2, 8, TOK, DQ), BF),
        pltpu.VMEM((2, 8, TOK, DQ), BF),
        pltpu.VMEM((TOK, NX * DQ), BF),
        pltpu.VMEM((TOK, DQ), F32),
        pltpu.VMEM((NY - 1, TOK, DQ), BF),
        pltpu.VMEM((NY - 1, TOK, DQ), BF),
        pltpu.SemaphoreType.DMA((252,)),
        pltpu.SemaphoreType.DMA((252,)),
        pltpu.SemaphoreType.DMA((20,)),
    ]
    return pl.pallas_call(
        kernel,
        out_shape=jax.ShapeDtypeStruct((TOK, DQ), BF),
        in_specs=[anywhere, vmem, vmem, vmem, anywhere, anywhere, anywhere, anywhere, vmem],
        out_specs=vmem,
        scratch_shapes=scratch,
        compiler_params=pltpu.CompilerParams(
            collective_id=0, has_side_effects=True, vmem_limit_bytes=60 * 1024 * 1024
        ),
        cost_estimate=pl.CostEstimate(flops=8_000_000_000, bytes_accessed=8_000_000, transcendentals=400_000),
    )(
        grad_out, expert_ids.T, gate_values.T, shared_down.T, shared_gate_up, saved_gate_up, expert_gate_up, expert_down,
        shared_saved,
    )


def solution(mesh):
    in_specs = (
        P("ep", None),
        P("ep", None),
        P("ep", None),
        P("ep", None, None, "tp"),
        P("ep", None, None, "tp"),
        P("ep", "tp", None),
        P(None, "ep", "tp"),
        P(None, "ep", "tp"),
        P("tp", "ep"),
    )
    return jax.shard_map(shards, mesh=mesh, in_specs=in_specs, out_specs=P("ep", "tp"), check_vma=False)
```

```python
import functools

import jax
import jax.numpy as jnp
from jax import lax
from jax.experimental import pallas as pl
from jax.experimental.pallas import tpu as pltpu
from jax.sharding import PartitionSpec as P

BF = jnp.bfloat16
F32 = jnp.float32
NX, NZ, NC, NY = 4, 16, 2, 4
PEERS = NX * NC
TOK = 128
CAP = 6
TOP = 10
DQ = 512
HQ = 128
NE = 2
GROUPS = 4
SPAN = NZ // GROUPS
SROWS = SPAN * CAP
QN = PEERS * NE
PR = NE * SROWS
ROWS = PEERS * PR
HOME = 0
AGC = 4
AGR = TOK // AGC
RSC = 2
RSR = TOK // RSC
OFFS = (0, 1, -1, 2, -2, 3, -3, 4, -4, 5, -5, 6, -6, 7, -7, 8)


def dot_nt(a, b):
    return lax.dot_general(a, b, (((1,), (1,)), ((), ())), preferred_element_type=F32)


def dot_nn(a, b):
    return lax.dot_general(a, b, (((1,), (0,)), ((), ())), preferred_element_type=F32)


def dot_tn(a, b):
    return lax.dot_general(a, b, (((0,), (0,)), ((), ())), preferred_element_type=F32)


def act_grad(h, g, u):
    g = g.astype(F32)
    u = u.astype(F32)
    s = jax.nn.sigmoid(g)
    return (h * u * s * (1.0 + g * (1.0 - s))).astype(BF), (h * g * s).astype(BF)


def kernel(
    x_in, ids, gates, sd, sgu, saved, gu, down, ssaved, out,
    XG, MG, SW, SEL, WTH, WTL, SB, R1, W1, W2, SVI, SVP, HO, HS, HR, G, OB, BK, PT, ZS, ZR, XF, SHO, SP, SR,
    ssem, rsem, lsem,
):
    ep = lax.axis_index("ep")
    y = lax.axis_index("tp")
    c = lax.rem(ep, NC)
    z = lax.rem(lax.div(ep, NC), NZ)
    x = lax.div(ep, NC * NZ)
    me = x * NC + c

    def zdev(off):
        return ((x * NZ + lax.rem(z + off + NZ, NZ)) * NC + c, y)

    def pdev(peer):
        return ((lax.div(peer, NC) * NZ + z) * NC + lax.rem(peer, NC), y)

    def peer_of(d):
        return lax.rem(me + d + PEERS, PEERS)

    def yof(d):
        return lax.rem(y + d + NY, NY)

    def ydev(d):
        return (ep, yof(d))

    counts = {"s": 0, "r": 0, "l": 0}
    pending = []

    def rsem_new():
        counts["r"] += 1
        return rsem.at[counts["r"] - 1]

    def send(src, dst, rs, dev):
        ss = ssem.at[counts["s"]]
        counts["s"] += 1
        cp = pltpu.make_async_remote_copy(
            src_ref=src, dst_ref=dst, send_sem=ss, recv_sem=rs, device_id=dev,
            device_id_type=pl.DeviceIdType.MESH,
        )
        cp.start()
        pending.append(cp)

    def recv(dst, rs):
        pltpu.make_async_remote_copy(
            src_ref=dst, dst_ref=dst, send_sem=rs, recv_sem=rs, device_id=(ep, y),
            device_id_type=pl.DeviceIdType.MESH,
        ).wait_recv()

    def local(src, dst):
        cp = pltpu.make_async_copy(src, dst, lsem.at[counts["l"]])
        counts["l"] += 1
        cp.start()
        return cp

    barrier = pltpu.get_barrier_semaphore()
    others = [zdev(1), zdev(-1)] + [pdev(peer_of(d)) for d in range(1, PEERS)] + [ydev(d) for d in range(1, NY)]
    for dev in others:
        pl.semaphore_signal(barrier, inc=1, device_id=dev, device_id_type=pl.DeviceIdType.MESH)
    mine = pl.ds(pl.multiple_of(y * DQ, DQ), DQ)
    cp_x = local(x_in.at[:, mine], XG.at[HOME])
    cp_s = local(sgu, SW.at[pl.ds(1, 2), x, z, c])
    cp_sv = [local(saved.at[e, k], SVI.at[:, pl.ds((2 * e + k) * HQ, HQ)]) for e in range(NE) for k in range(2)]
    cp_w1 = local(down.at[:, :, mine], W1.at[:, pl.ds(pl.multiple_of(y * HQ, HQ), HQ), :])
    cp_w2 = local(gu.at[:, :, mine, :], W2.at[:, y])
    cp_xf = local(x_in, XF)
    pl.semaphore_wait(barrier, len(others))

    def slot(off):
        return OFFS.index(8 if off == -8 else off)

    ag_sems = {}
    SWI = AGC + 1

    def ag_ref(s, direction, i):
        off = -s if direction == 0 else s
        k = slot(off)
        if s == 8 and (i in (0, SWI) or 1 <= i <= AGC // 2) != (direction == 0):
            return None
        if i == 0:
            return MG.at[k]
        if i == SWI:
            return SW.at[:, x, lax.rem(z + off + NZ, NZ), c]
        return XG.at[k, pl.ds((i - 1) * AGR, AGR), :]

    def ag_send(s, direction, i):
        there = ag_ref(s, direction, i)
        if there is None:
            return
        off = -s if direction == 0 else s
        k = slot(off)
        src = ag_ref(s - 1, direction, i) if s < 9 else None
        if i == 0:
            dst = MG.at[k]
        elif i == SWI:
            dst = src
        else:
            dst = XG.at[k, pl.ds((i - 1) * AGR, AGR), :]
            if s == 1:
                src = x_in.at[pl.ds((i - 1) * AGR, AGR), mine]
        rs = rsem_new()
        ag_sems[(s, direction, i)] = rs
        send(src, dst, rs, zdev(1 if direction == 0 else -1))

    MG[HOME, 0:TOP] = ids[...].astype(F32)
    MG[HOME, TOP:2 * TOP] = gates[...]
    MG[HOME, 2 * TOP:24] = jnp.zeros((24 - 2 * TOP, TOK), F32)
    SW[0, x, z, c] = sd[...]
    w1_sems, w2_sems = {}, {}

    def send_w1():
        for d in range(1, NY):
            w1_sems[d] = rsem_new()
            there = pl.ds(pl.multiple_of(yof(d) * DQ, DQ), DQ)
            send(down.at[:, :, there], W1.at[:, pl.ds(pl.multiple_of(y * HQ, HQ), HQ), :], w1_sems[d], ydev(d))

    def send_w2():
        for d in range(1, NY):
            w2_sems[d] = rsem_new()
            there = pl.ds(pl.multiple_of(yof(d) * DQ, DQ), DQ)
            send(gu.at[:, :, there, :], W2.at[:, y], w2_sems[d], ydev(d))

    for direction in range(2):
        ag_send(1, direction, 0)
    send_w1()
    for i in range(1, AGC + 1):
        for direction in range(2):
            ag_send(1, direction, i)
    cp_s.wait()
    for direction in range(2):
        ag_send(1, direction, SWI)

    for cp in cp_sv:
        cp.wait()

    def second(width):
        return lax.broadcasted_iota(jnp.int32, (PEERS, PR, width), 1).reshape(ROWS, width) >= SROWS

    def permute_saved(g):
        shape = (PEERS, PR, NZ * PEERS * CAP)
        src = lax.broadcasted_iota(jnp.int32, shape, 0)
        i = lax.broadcasted_iota(jnp.int32, shape, 1)
        lane = lax.broadcasted_iota(jnp.int32, shape, 2)
        i = jnp.where(i >= SROWS, i - SROWS, i)
        j = lax.shift_right_logical(i * 43, 8)
        offs = [(o + NZ) % NZ for o in OFFS[g * SPAN:(g + 1) * SPAN]]
        off = jnp.where(j == 0, offs[0], jnp.where(j == 1, offs[1], jnp.where(j == 2, offs[2], offs[3])))
        zz = (z + off) & (NZ - 1)
        target = lax.shift_right_logical(src, 1) * (NZ * NC * CAP) + zz * (NC * CAP) + (src & 1) * CAP + (i - j * CAP)
        pick = jnp.where(target == lane, 1.0, 0.0).astype(BF).reshape(ROWS, NZ * PEERS * CAP)
        got = dot_nn(pick, SVI[...])
        SVP[g] = jnp.where(second(2 * HQ), got[:, 2 * HQ:], got[:, :2 * HQ]).astype(BF)

    qi = lax.broadcasted_iota(jnp.int32, (QN, TOK), 0)
    expert = (lax.shift_right_logical(qi, 2) * (NZ * NC * NE) + z * (NC * NE) + (qi & 3)).astype(F32)
    before = jnp.where(
        lax.broadcasted_iota(jnp.int32, (TOK, TOK), 0) < lax.broadcasted_iota(jnp.int32, (TOK, TOK), 1), 1.0, 0.0
    ).astype(BF)
    row3 = lax.broadcasted_iota(jnp.int32, (QN, SROWS, TOK), 1).astype(F32)
    lane_q = lax.broadcasted_iota(jnp.int32, (QN, QN * SROWS), 1)
    row_q = lax.broadcasted_iota(jnp.int32, (QN, QN * SROWS), 0)
    in_q = (lane_q >= row_q * SROWS) & (lane_q < row_q * SROWS + SROWS)
    spread = jnp.where(in_q, 1.0, 0.0).astype(BF)
    lane_i = jnp.sum(jnp.where(in_q, lane_q - row_q * SROWS, 0).astype(F32), axis=0, keepdims=True)

    def place(k):
        meta = MG[k]
        named = jnp.zeros((QN, TOK), F32)
        gate = jnp.zeros((QN, TOK), F32)
        for i in range(TOP):
            hit = meta[i:i + 1, :] == expert
            named = jnp.where(hit, 1.0, named)
            gate = jnp.where(hit, meta[TOP + i:TOP + i + 1, :], gate)
        rank = dot_nn(named.astype(BF), before)
        key = jnp.where(named > 0.5, rank + float((k % SPAN) * CAP), -1.0)
        return key, gate

    x_sems, b_sems = {}, {}

    def select(g):
        for j in range(SPAN):
            key, gate = place(g * SPAN + j)
            hot = jnp.where(key[:, None, :] == row3, 1.0, 0.0).reshape(QN * SROWS, TOK)
            SEL[:, pl.ds(j * TOK, TOK)] = hot.astype(BF)
        rows = XG[g * SPAN:(g + 1) * SPAN].reshape(SPAN * TOK, DQ)
        SB[g] = dot_nn(SEL[...], rows).astype(BF).reshape(PEERS, PR, DQ)
        for d in range(1, PEERS):
            rs = rsem_new()
            x_sems[(g, d)] = rs
            peer = peer_of(d)
            send(SB.at[g, peer], R1.at[g, me], rs, pdev(peer))
        return local(SB.at[g, me], R1.at[g, me])

    def weigh(g):
        for j in range(SPAN):
            key, gate = place(g * SPAN + j)
            high = gate.astype(BF)
            low = (gate - high.astype(F32)).astype(BF)
            where = dot_tn(key.astype(BF), spread) == lane_i
            at = pl.ds(j * TOK, TOK)
            WTH[g, at, :] = jnp.where(where, dot_tn(high, spread), 0.0).astype(BF)
            WTL[g, at, :] = jnp.where(where, dot_tn(low, spread), 0.0).astype(BF)

    keep, sw_sems, h_sems, g_sems = {}, {}, {}, {}

    def spread_shared():
        for d in range(1, PEERS):
            sw_sems[d] = rsem_new()
            part = SW.at[:, x, :, c]
            send(part, part, sw_sems[d], pdev(peer_of(d)))

    def wait_w1():
        cp_w1.wait()
        for d in range(1, NY):
            recv(W1.at[:, pl.ds(pl.multiple_of(yof(-d) * HQ, HQ), HQ), :], w1_sems[d])

    def wait_w2():
        cp_w2.wait()
        for d in range(1, NY):
            recv(W2.at[:, yof(-d)], w2_sems[d])

    def hidden(g):
        keep[g].wait()
        for d in range(1, PEERS):
            recv(R1.at[g, peer_of(-d)], x_sems[(g, d)])
        rows = R1[g].reshape(ROWS, DQ)
        mine_second = second(HQ)
        for d in (1, 2, 3, 0):
            quarter = pl.ds(pl.multiple_of(yof(d) * HQ, HQ), HQ)
            both = dot_nt(rows, jnp.concatenate([W1[e, quarter, :] for e in range(NE)], axis=0))
            part = jnp.where(mine_second, both[:, HQ:], both[:, :HQ])
            if d == 0:
                HO[g] = part
            else:
                HS[g, d - 1] = part.astype(BF)
                rs = rsem_new()
                h_sems[(g, d)] = rs
                send(HS.at[g, d - 1], HR.at[g, d - 1], rs, ydev(d))

    def activate(g):
        h = HO[g]
        for d in range(1, NY):
            recv(HR.at[g, d - 1], h_sems[(g, d)])
            h = h + HR[g, d - 1].astype(F32)
        a, b = act_grad(h, SVP[g, :, pl.ds(0, HQ)], SVP[g, :, pl.ds(HQ, HQ)])
        G[g, y, 0] = a
        G[g, y, 1] = b
        for d in (1, -1):
            rs = rsem_new()
            g_sems[(g, d)] = rs
            send(G.at[g, y], G.at[g, y], rs, ydev(d))

    def relay(g):
        for k, d in ((0, 1), (1, -1)):
            piece = G.at[g, yof(-d)]
            recv(piece, g_sems[(g, d)])
            rs = rsem_new()
            g_sems[(g, 2, k)] = rs
            send(piece.at[k], piece.at[k], rs, ydev(d))

    def outward(g):
        for k in range(2):
            recv(G.at[g, yof(2), k], g_sems[(g, 2, k)])
        left = jnp.concatenate([G[g, q, k] for q in range(NY) for k in range(2)], axis=1)
        parts = []
        for e in range(NE):
            right = jnp.concatenate([W2[e, q, k] for q in range(NY) for k in range(2)], axis=1)
            parts.append(dot_nt(left, right))
        OB[g] = jnp.where(second(DQ), parts[1], parts[0]).astype(BF).reshape(PEERS, PR, DQ)
        for d in range(1, PEERS):
            rs = rsem_new()
            b_sems[(g, d)] = rs
            peer = peer_of(d)
            send(OB.at[g, peer], BK.at[g, me], rs, pdev(peer))
        keep[g + GROUPS] = local(OB.at[g, me], BK.at[g, me])

    def combine(g):
        keep[g + GROUPS].wait()
        for d in range(1, PEERS):
            recv(BK.at[g, peer_of(-d)], b_sems[(g, d)])
        rows = BK[g].reshape(ROWS, DQ)
        got = dot_nn(WTH[g], rows) + dot_nn(WTL[g], rows)
        PT[g * SPAN:(g + 1) * SPAN] = got.reshape(SPAN, TOK, DQ)

    s_sems = {}

    def shared_products():
        cp_xf.wait()
        for d in range(1, PEERS):
            peer = peer_of(-d)
            recv(SW.at[:, lax.div(peer, NC), :, lax.rem(peer, NC)], sw_sems[d])
        h = dot_nn(XF[...], SW[0].reshape(NX * DQ, HQ))
        a, b = act_grad(h, ssaved[0], ssaved[1])
        for d in list(range(1, NY)) + [0]:
            q = yof(d)
            part = dot_nt(a, SW[1, q].reshape(DQ, HQ)) + dot_nt(b, SW[2, q].reshape(DQ, HQ))
            if d == 0:
                SHO[...] = part
            else:
                SP[d - 1] = part.astype(BF)

    def shared_sum():
        for d in range(1, NY):
            s_sems[d] = rsem_new()
            send(SP.at[d - 1], SR.at[d - 1], s_sems[d], ydev(d))

    z_sems = {}

    def rs_step(s):
        for i in range(RSC):
            rows = pl.ds(i * RSR, RSR)
            for direction in range(2):
                if s == 1 and (i < RSC // 2) != (direction == 0):
                    continue
                off = 9 - s if direction == 0 else s - 9
                part = PT[slot(off), rows, :]
                if (s - 1, direction, i) in z_sems:
                    recv(ZR.at[direction, s - 2, rows, :], z_sems[(s - 1, direction, i)])
                    part = part + ZR[direction, s - 2, rows, :].astype(F32)
                ZS[direction, s - 1, rows, :] = part.astype(BF)
                rs = rsem_new()
                z_sems[(s, direction, i)] = rs
                send(
                    ZS.at[direction, s - 1, rows, :], ZR.at[direction, s - 1, rows, :], rs,
                    zdev(1 if direction == 0 else -1),
                )

    cp_x.wait()
    for s in range(1, 9):
        for i in range(AGC + 2):
            for direction in range(2):
                ref = ag_ref(s, direction, i)
                if ref is None:
                    continue
                recv(ref, ag_sems[(s, direction, i)])
                if s < 8:
                    ag_send(s + 1, direction, i)
        if s == 1:
            permute_saved(0)
        if s == 2:
            keep[0] = select(0)
            send_w2()
        if s == 3:
            permute_saved(1)
        if s == 4:
            keep[1] = select(1)
        if s == 5:
            wait_w1()
            hidden(0)
        if s == 6:
            keep[2] = select(2)
        if s == 7:
            hidden(1)
    keep[3] = select(3)
    hidden(2)
    permute_saved(3)
    weigh(3)
    hidden(3)
    spread_shared()
    permute_saved(2)
    activate(3)
    weigh(2)
    weigh(1)
    relay(3)
    activate(2)
    wait_w2()
    outward(3)
    relay(2)
    activate(1)
    weigh(0)
    combine(3)
    rs_step(1)
    outward(2)
    relay(1)
    activate(0)
    rs_step(2)
    combine(2)
    rs_step(3)
    outward(1)
    relay(0)
    rs_step(4)
    combine(1)
    rs_step(5)
    outward(0)
    shared_products()
    shared_sum()
    rs_step(6)
    combine(0)
    rs_step(7)
    rs_step(8)
    total = PT[HOME] + SHO[...]
    for d in range(1, NY):
        recv(SR.at[d - 1], s_sems[d])
        total = total + SR[d - 1].astype(F32)
    PT[HOME] = total
    for i in range(RSC):
        rows = pl.ds(i * RSR, RSR)
        part = PT[HOME, rows, :]
        for direction in range(2):
            recv(ZR.at[direction, 7, rows, :], z_sems[(8, direction, i)])
            part = part + ZR[direction, 7, rows, :].astype(F32)
        out[rows, :] = part.astype(BF)
    for cp in pending:
        cp.wait_send()


def shards(
    grad_out, expert_ids, gate_values, saved_gate_up, expert_gate_up, expert_down,
    shared_saved, shared_gate_up, shared_down,
):
    anywhere = pl.BlockSpec(memory_space=pl.ANY)
    vmem = pl.BlockSpec(memory_space=pltpu.VMEM)
    slots = NZ * PEERS * CAP
    scratch = [
        pltpu.VMEM((NZ, TOK, DQ), BF),
        pltpu.VMEM((NZ, 24, TOK), F32),
        pltpu.VMEM((3, NX, NZ, NC, 16, HQ), BF),
        pltpu.VMEM((ROWS, SPAN * TOK), BF),
        pltpu.VMEM((GROUPS, SPAN * TOK, ROWS), BF),
        pltpu.VMEM((GROUPS, SPAN * TOK, ROWS), BF),
        pltpu.VMEM((GROUPS, PEERS, PR, DQ), BF),
        pltpu.VMEM((GROUPS, PEERS, PR, DQ), BF),
        pltpu.VMEM((NE, NY * HQ, DQ), BF),
        pltpu.VMEM((NE, NY, 2, DQ, HQ), BF),
        pltpu.VMEM((slots, 2 * NE * HQ), BF),
        pltpu.VMEM((GROUPS, ROWS, 2 * HQ), BF),
        pltpu.VMEM((GROUPS, ROWS, HQ), F32),
        pltpu.VMEM((GROUPS, NY - 1, ROWS, HQ), BF),
        pltpu.VMEM((GROUPS, NY - 1, ROWS, HQ), BF),
        pltpu.VMEM((GROUPS, NY, 2, ROWS, HQ), BF),
        pltpu.VMEM((GROUPS, PEERS, PR, DQ), BF),
        pltpu.VMEM((GROUPS, PEERS, PR, DQ), BF),
        pltpu.VMEM((NZ, TOK, DQ), F32),
        pltpu.VMEM((2, 8, TOK, DQ), BF),
        pltpu.VMEM((2, 8, TOK, DQ), BF),
        pltpu.VMEM((TOK, NX * DQ), BF),
        pltpu.VMEM((TOK, DQ), F32),
        pltpu.VMEM((NY - 1, TOK, DQ), BF),
        pltpu.VMEM((NY - 1, TOK, DQ), BF),
        pltpu.SemaphoreType.DMA((252,)),
        pltpu.SemaphoreType.DMA((252,)),
        pltpu.SemaphoreType.DMA((20,)),
    ]
    return pl.pallas_call(
        kernel,
        out_shape=jax.ShapeDtypeStruct((TOK, DQ), BF),
        in_specs=[anywhere, vmem, vmem, vmem, anywhere, anywhere, anywhere, anywhere, vmem],
        out_specs=vmem,
        scratch_shapes=scratch,
        compiler_params=pltpu.CompilerParams(
            collective_id=0, has_side_effects=True, vmem_limit_bytes=60 * 1024 * 1024
        ),
        cost_estimate=pl.CostEstimate(flops=8_000_000_000, bytes_accessed=8_000_000, transcendentals=400_000),
    )(
        grad_out, expert_ids.T, gate_values.T, shared_down.T, shared_gate_up, saved_gate_up, expert_gate_up, expert_down,
        shared_saved,
    )


def solution(mesh):
    in_specs = (
        P("ep", None),
        P("ep", None),
        P("ep", None),
        P("ep", None, None, "tp"),
        P("ep", None, None, "tp"),
        P("ep", "tp", None),
        P(None, "ep", "tp"),
        P(None, "ep", "tp"),
        P("tp", "ep"),
    )
    return jax.shard_map(shards, mesh=mesh, in_specs=in_specs, out_specs=P("ep", "tp"), check_vma=False)
```
